32 devices in a mesh: dp: 4 (over y, x), expert: 8 (over z, core).
Axes of the slice: x: 2, y: 2, z: 4, core: 2. Of those that a mesh axis runs over, the one named last changes fastest.
Arguments:
- tokens: bfloat16 [4096, 2048], P(('dp', 'expert')), may hold values from -6 to 6
- out_grad: bfloat16 [4096, 2048], P(('dp', 'expert')), may hold values from -6 to 6
- expert_ids: int32 [4096, 8], P(('dp', 'expert')), may hold values from 0 to 15, all different within a row; in each aligned block of 128 rows (0 to 127, 128 to 255, ...) at most 72 rows name the same one
- route_probs: float32 [4096, 8], P(('dp', 'expert')), may hold values from 0.05 to 0.5
- gate_weight: bfloat16 [16, 2048, 384], P('expert'), may hold values from -0.125 to 0.125
- up_weight: bfloat16 [16, 2048, 384], P('expert'), may hold values from -0.125 to 0.125
- down_weight: bfloat16 [16, 384, 2048], P('expert'), may hold values from -0.3125 to 0.3125
Outputs:
- in_grad: bfloat16 [4096, 2048], P(('dp', 'expert'))
- grad_gate: bfloat16 [16, 2048, 384], P('expert', 'dp')
- grad_up: bfloat16 [16, 2048, 384], P('expert', 'dp')
- grad_down: bfloat16 [16, 384, 2048], P('expert', None, 'dp')
The draws below stay inside these ranges and needn't reach their ends.
Inputs may be any that keep to these rules, and one draw needn't show every extreme that they name: `expert_ids`: within the 128 tokens of one device no expert is named more than 72 times, a bound that some block reaches; a token names 8 different experts.
All inputs are finite; a program needn't handle non-finite values.
Results may differ from the reference program's by a relative error of at most 0.014.
Values may be sent and summed in bfloat16 or wider, within the bound.
A program may use at most 128 MiB of HBM per device.

```python
import math
import jax
import jax.numpy as jnp
import numpy as np
from jax import lax

D = 2048
HID = 384
TOP = 8
TOK_DEV = 128
EXPERTS = 16
CAP = 72
TOKENS = 4096
N_DP = 4
N_EXPERT = 8


def spiked(result, rng, source, target, blocks, factor):
    owner, partner = [(jnp.arange(result.shape[position]) // (result.shape[position] // blocks)).reshape([-1 if axis == position else 1 for axis in range(result.ndim)]) for position in (source, target)]
    chosen = jax.random.permutation(rng, blocks)[partner]
    strong = (owner == chosen) | (owner == (partner + blocks // 2) % blocks)
    return jnp.where(strong, factor * result, result)


def block_levels(stream_key, dims, split, smallest, top_value):
    def one(axis_at, blocks):
        heights = jax.random.uniform(jax.random.fold_in(jax.random.fold_in(stream_key, 6), axis_at), (blocks,), jnp.float32, smallest / len(split), top_value / len(split))
        return jnp.repeat(jnp.exp(heights), dims[axis_at] // blocks).reshape((-1,) + (1,) * (len(dims) - axis_at - 1))

    gain = one(*split[0])
    for cut in split[1:]:
        gain = gain * one(*cut)
    return gain


def routed_block(key, own, number, rows, number_of, top, reach, slope):
    ranking = jax.random.permutation(key, number_of)
    packed, usual = load_shares(number_of, rows * top, reach, slope, True), load_shares(number_of, rows * top, reach, slope, False)
    places = jnp.arange(number_of)

    def named(lengths, offset_by):
        used = int((lengths > 0).sum())
        fixed = max(1, used // 4)
        passed = fixed + (places - fixed + offset_by * (used - fixed)) % max(1, number_of - fixed)
        return jnp.zeros((number_of,), jnp.int32).at[ranking[jnp.where(places < fixed, places, passed)]].set(jnp.asarray(lengths, jnp.int32))

    lengths = jnp.where(number % 4 == 0, named(packed, number // 4), named(usual, number - number // 4 - 1))
    mixed = jax.random.permutation(jax.random.fold_in(own, 3), number_of)
    source_of, taker = mixed[0:number_of // 2 * 2:2], mixed[1:number_of // 2 * 2:2]
    room = jnp.minimum(lengths[source_of] - 1, reach - lengths[taker]) // 2
    room = jnp.where((source_of == ranking[0]) | (taker == ranking[0]) | (lengths[taker] == 0), 0, jnp.maximum(room, 0))
    passed = jax.random.randint(jax.random.fold_in(own, 4), (number_of // 2,), 0, 1 << 20) % (room + 1)
    lengths = lengths.at[source_of].add(-passed).at[taker].add(passed)
    members = jnp.searchsorted(jnp.cumsum(lengths), jnp.arange(rows * top), side="right").astype(jnp.int32)
    grid = members.reshape(top, rows).T
    grid = grid[jax.random.permutation(jax.random.fold_in(own, 1), rows)]
    offset_by = jax.random.randint(jax.random.fold_in(own, 2), (rows, 1), 0, top)
    return jnp.take_along_axis(grid, (jnp.arange(top)[None, :] + offset_by) % top, axis=1)


def load_shares(count, total, most, slope, full):
    weights = [(1 << 20) // math.isqrt(standing ** slope) + 1 for standing in range(1, count + 1)]
    largest = most if full else min(most, max(-(-total // count), total * weights[0] // sum(weights)))
    least = 1 if total - largest >= count - 1 else 0
    given, rest = [largest] + [least] * (count - 1), total - largest - least * (count - 1)
    while rest > 0:
        movable = [i for i in range(1, count) if given[i] < largest] or [i for i in range(1, count) if given[i] < most]
        whole, left = sum([weights[i] for i in movable]), rest
        for i in movable:
            addition = min(most - given[i], max(1, left * weights[i] // whole), rest)
            given[i] = given[i] + addition
            rest = rest - addition
    return np.array(given)


def scatter_about(stream_key, dims, width, limit, pieces=(), held_as=jnp.bfloat16):
    drawn = width * jax.random.normal(stream_key, dims, jnp.float32)
    if pieces:
        drawn = drawn * block_levels(stream_key, dims, pieces, -0.22, 0.18)
    return jnp.clip(drawn, -limit, limit).astype(held_as)


def noise_with(key, shape, width, most, shards, heavy, held_as=jnp.bfloat16):
    result = width * jax.random.normal(key, shape, jnp.float32)
    if shards:
        result = result * block_levels(key, shape, shards, -0.22, 0.18)
    return jnp.clip(spiked(result, jax.random.fold_in(key, 3), *heavy), -most, most).astype(held_as)


def setup_inputs(seed: int = 0) -> dict:
    seeds = jax.random.split(jax.random.key(seed), 8)
    tokens = noise_with(seeds[0], (TOKENS, D), 1.0, 6.0, ((0, 32),), (0, 1, 32, 2.75))
    out_grad = scatter_about(seeds[1], (TOKENS, D), 1.0, 6.0, ((0, 32),))
    expert_ids_keys = jax.random.split(jax.random.fold_in(seeds[2], 1), TOKENS // TOK_DEV)
    expert_ids_turns = jax.random.permutation(jax.random.fold_in(seeds[2], 3), TOKENS // TOK_DEV)
    expert_ids = jax.vmap(lambda own, number: routed_block(jax.random.fold_in(seeds[2], 2), own, number, TOK_DEV, EXPERTS, TOP, CAP, 2))(expert_ids_keys, expert_ids_turns).reshape((TOKENS, TOP))
    route_probs = jnp.clip(jnp.exp(math.log(0.5) - 2.3025851 * jax.random.uniform(seeds[3], (TOKENS, TOP), jnp.float32) ** block_levels(seeds[3], (TOKENS, TOP), ((0, 32),), -0.2, 0.2)), 0.05, 0.5)
    gate_weight = scatter_about(seeds[4], (EXPERTS, D, HID), D ** -0.5, 0.125, ((0, 8),))
    up_weight = scatter_about(seeds[5], (EXPERTS, D, HID), D ** -0.5, 0.125, ((0, 8),))
    down_weight = scatter_about(seeds[6], (EXPERTS, HID, D), HID ** -0.5, 0.3125, ((0, 8),))
    return dict(tokens=tokens, out_grad=out_grad, expert_ids=expert_ids, route_probs=route_probs, gate_weight=gate_weight, up_weight=up_weight, down_weight=down_weight)


def reference(tokens, out_grad, expert_ids, route_probs, gate_weight, up_weight, down_weight):
    blocks = N_DP * N_EXPERT
    pairs = TOK_DEV * TOP
    flat = expert_ids.reshape(blocks, pairs)
    columns = jnp.arange(EXPERTS, dtype=jnp.int32)
    onehot = (flat[:, :, None] == columns[None, None, :]).astype(jnp.int32)
    rank = jnp.sum(jnp.cumsum(onehot, axis=1) * onehot, axis=2) - 1
    slot = (flat * CAP + rank).astype(jnp.int32)
    block_ids = jnp.arange(blocks, dtype=jnp.int32)[:, None]
    local_ids = jnp.broadcast_to(jnp.arange(pairs, dtype=jnp.int32)[None, :], (blocks, pairs))
    table = jnp.full((blocks, EXPERTS * CAP), pairs, dtype=jnp.int32)
    table = table.at[jnp.broadcast_to(block_ids, (blocks, pairs)), slot].set(local_ids)
    glob = jnp.where(table < pairs, table + block_ids * pairs, blocks * pairs).astype(jnp.int32)
    table_e = glob.reshape(blocks, EXPERTS, CAP).transpose(1, 0, 2).reshape(EXPERTS, blocks * CAP)
    zero_row = jnp.zeros((1, D), dtype=jnp.bfloat16)
    x_pad = jnp.concatenate([tokens, zero_row], axis=0)
    dy_pad = jnp.concatenate([out_grad, zero_row], axis=0)
    p_pad = jnp.concatenate([route_probs.reshape(-1), jnp.zeros((1,), dtype=jnp.float32)], axis=0)

    def group_sum(left, right):
        lf = left.astype(jnp.float32).reshape(N_DP, N_EXPERT * CAP, left.shape[1])
        rf = right.astype(jnp.float32).reshape(N_DP, N_EXPERT * CAP, right.shape[1])
        parts = jnp.einsum("prd,prh->pdh", lf, rf).astype(jnp.bfloat16)
        return jnp.sum(parts.astype(jnp.float32), axis=0).astype(jnp.bfloat16)

    def one_expert(carry, inputs):
        rows, w_gate, w_up, w_down = inputs
        tok = (rows // TOP).astype(jnp.int32)
        xr = x_pad[tok]
        scaled = (p_pad[rows][:, None] * dy_pad[tok].astype(jnp.float32)).astype(jnp.bfloat16)
        gate = jnp.dot(xr, w_gate, preferred_element_type=jnp.float32)
        up = jnp.dot(xr, w_up, preferred_element_type=jnp.float32)
        sig = jax.nn.sigmoid(gate)
        act = (gate * sig * up).astype(jnp.bfloat16)
        dh = jnp.dot(scaled, w_down.T, preferred_element_type=jnp.float32)
        dgate = (dh * up * sig * (1.0 + gate * (1.0 - sig))).astype(jnp.bfloat16)
        dup = (dh * gate * sig).astype(jnp.bfloat16)
        contrib = (jnp.dot(dgate, w_gate.T, preferred_element_type=jnp.float32)
                   + jnp.dot(dup, w_up.T, preferred_element_type=jnp.float32)).astype(jnp.bfloat16)
        carry = carry.at[tok].add(contrib.astype(jnp.float32))
        grad_g = group_sum(xr, dgate)
        grad_u = group_sum(xr, dup)
        grad_d = group_sum(act, scaled)
        return carry, (grad_g, grad_u, grad_d)

    start = jnp.zeros((TOKENS + 1, D), dtype=jnp.float32)
    total, grads = lax.scan(one_expert, start, (table_e, gate_weight, up_weight, down_weight))
    in_grad = total[:TOKENS].astype(jnp.bfloat16)
    return (in_grad, grads[0], grads[1], grads[2])
```

```python
import jax
import jax.numpy as jnp
from jax import lax
from jax.sharding import PartitionSpec as P


def contract(left, right, left_dim, right_dim):
    return lax.dot_general(
        left, right, (((left_dim,), (right_dim,)), ((), ())), preferred_element_type=jnp.float32
    )


def per_device(tokens, out_grad, expert_ids, route_probs, gate_weight, up_weight, down_weight):
    width = tokens.shape[1]
    exp_dev, _, hid = gate_weight.shape
    bf16 = jnp.bfloat16
    n_owner = lax.axis_size("expert")
    experts = exp_dev * n_owner
    columns = jnp.arange(experts, dtype=jnp.int32)
    hit = expert_ids[:, :, None] == columns[None, None, :]
    weight = jnp.sum(jnp.where(hit, route_probs[:, :, None], 0.0), axis=1)
    first = lax.axis_index("expert") * exp_dev
    all_weight = lax.all_gather(weight, "expert", axis=0, tiled=True)
    mine = lax.dynamic_slice_in_dim(all_weight, first, exp_dev, axis=1)
    x = lax.all_gather(tokens, "expert", axis=0, tiled=True)
    dy = lax.all_gather(out_grad, "expert", axis=0, tiled=True)
    w_gate = jnp.concatenate([gate_weight[e] for e in range(exp_dev)], axis=1)
    w_up = jnp.concatenate([up_weight[e] for e in range(exp_dev)], axis=1)
    w_down = down_weight.reshape(exp_dev * hid, width)
    prob = jnp.repeat(mine, hid, axis=1)
    gate = contract(x, w_gate, 1, 0)
    up = contract(x, w_up, 1, 0)
    sig = jax.nn.sigmoid(gate)
    silu = gate * sig
    slope = up * sig * (1.0 + gate * (1.0 - sig))
    dh = contract(dy, w_down, 1, 1) * prob
    act = (silu * up * prob).astype(bf16)
    dgate = (dh * slope).astype(bf16)
    dup = (dh * silu).astype(bf16)
    grad_d = contract(act, dy, 0, 0).astype(bf16).reshape(exp_dev, hid, width)
    grad_g = contract(x, dgate, 0, 0).astype(bf16)
    grad_u = contract(x, dup, 0, 0).astype(bf16)
    grad_g = jnp.stack([grad_g[:, e * hid:(e + 1) * hid] for e in range(exp_dev)], axis=0)
    grad_u = jnp.stack([grad_u[:, e * hid:(e + 1) * hid] for e in range(exp_dev)], axis=0)
    part = (contract(dgate, w_gate, 1, 1) + contract(dup, w_up, 1, 1)).astype(bf16)
    in_grad = lax.psum_scatter(part, "expert", scatter_dimension=0, tiled=True)
    grad_d = lax.psum_scatter(grad_d, "dp", scatter_dimension=2, tiled=True)
    grad_g = lax.psum_scatter(grad_g, "dp", scatter_dimension=1, tiled=True)
    grad_u = lax.psum_scatter(grad_u, "dp", scatter_dimension=1, tiled=True)
    return (in_grad, grad_g, grad_u, grad_d)


def solution(mesh):
    in_specs = (
        P(("dp", "expert"), None),
        P(("dp", "expert"), None),
        P(("dp", "expert"), None),
        P(("dp", "expert"), None),
        P("expert", None, None),
        P("expert", None, None),
        P("expert", None, None),
    )
    out_specs = (
        P(("dp", "expert"), None),
        P("expert", "dp", None),
        P("expert", "dp", None),
        P("expert", None, "dp"),
    )
    return jax.shard_map(
        per_device, mesh=mesh, in_specs=in_specs, out_specs=out_specs, check_vma=False
    )
```

```python
import functools

import jax
import jax.numpy as jnp
from jax import lax
from jax.experimental import pallas as pl
from jax.experimental.pallas import tpu as pltpu
from jax.sharding import PartitionSpec as P


def contract(left, right, left_dim, right_dim):
    return lax.dot_general(
        left, right, (((left_dim,), (right_dim,)), ((), ())), preferred_element_type=jnp.float32
    )


MESH = pl.DeviceIdType.MESH


def ring_owner(place, n):
    return jnp.where(place < n // 2, 2 * place, 2 * (n - 1 - place) + 1)


def reduce_kernel(
    n, xt_ref, dy_ref, dgu_ref, actt_ref, w_ref,
    in_ref, out_gu, out_d,
    g_gu, g_d, r1_gu, r1_d, r2_gu, r2_d, part, landed,
    s1_send, s1_recv, s2_send, s2_recv, ring_send, ring_recv,
):
    f32, bf16 = jnp.float32, jnp.bfloat16
    me = lax.axis_index("dp")
    q = lax.axis_index("expert")
    xx, yy = me % 2, me // 2
    xn = yy * 2 + (1 - xx)
    yn = (1 - yy) * 2 + xx
    diag = 3 - me
    place = jnp.where(q % 2 == 0, q // 2, n - 1 - q // 2)
    right = ring_owner((place + 1) % n, n)
    left = ring_owner((place + n - 1) % n, n)

    barrier = pltpu.get_barrier_semaphore()
    for target in ((xn, q), (yn, q), (me, right), (me, left)):
        pl.semaphore_signal(barrier, inc=1, device_id=target, device_id_type=MESH)
    pl.semaphore_wait(barrier, 4)

    gu_rows, gu_cols = g_gu.shape[2:]
    d_rows, d_cols = g_d.shape[2:]
    tile = 512

    def weight_grads(block, half):
        rows = pl.multiple_of((block * 2 + half) * gu_rows, gu_rows)

        def step(i, carry):
            cols = pl.ds(pl.multiple_of(i * tile, tile), tile)
            g_gu[block, half, :, cols] = jnp.dot(
                xt_ref[pl.ds(rows, gu_rows), :], dgu_ref[:, cols], preferred_element_type=f32
            ).astype(bf16)
            return carry

        lax.fori_loop(0, gu_cols // tile, step, 0)
        g_d[block, half] = jnp.dot(
            actt_ref[pl.ds(half * d_rows, d_rows), :],
            dy_ref[:, pl.ds(pl.multiple_of(block * d_cols, d_cols), d_cols)],
            preferred_element_type=f32,
        ).astype(bf16)

    def first(block, half, slot):
        target = (xn, q) if half == 0 else (yn, q)
        copies = []
        for kind, (src, dst) in enumerate(((g_gu, r1_gu), (g_d, r1_d))):
            copies.append(pltpu.make_async_remote_copy(
                src_ref=src.at[block, half], dst_ref=dst.at[half, slot],
                send_sem=s1_send.at[half, slot, kind], recv_sem=s1_recv.at[half, slot, kind],
                device_id=target, device_id_type=MESH))
        return copies

    def second(block, half):
        target = (yn, q) if half == 0 else (xn, q)
        copies = []
        for kind, (src, dst) in enumerate(((g_gu, r2_gu), (g_d, r2_d))):
            copies.append(pltpu.make_async_remote_copy(
                src_ref=src.at[block, half], dst_ref=dst.at[half],
                send_sem=s2_send.at[half, kind], recv_sem=s2_recv.at[half, kind],
                device_id=target, device_id_type=MESH))
        return copies

    tok = in_ref.shape[0]
    hrow = tok // 2

    def ring_rows(s, way):
        if way == 0:
            owner = ring_owner((place + 2 * n - 1 - s) % n, n)
        else:
            owner = ring_owner((place + 1 + s) % n, n)
        return pl.ds(pl.multiple_of(owner * tok + way * hrow, hrow), hrow)

    def ring_copy(s, way):
        return pltpu.make_async_remote_copy(
            src_ref=part.at[ring_rows(s, way)], dst_ref=landed.at[way, s],
            send_sem=ring_send.at[way, s], recv_sem=ring_recv.at[way, s],
            device_id=(me, right if way == 0 else left), device_id_type=MESH)

    def ring_step(s):
        for way in range(2):
            if s > 0:
                ring_copy(s - 1, way).wait_recv()
                rows = ring_rows(s, way)
                part[rows] = (part[rows].astype(f32) + landed[way, s - 1].astype(f32)).astype(bf16)
            ring_copy(s, way).start()

    sends = []

    def go(copies):
        for copy in copies:
            copy.start()
        sends.extend(copies)

    weight_grads(diag, 0)
    first0 = first(diag, 0, 0)
    go(first0)
    weight_grads(diag, 1)
    first1 = first(diag, 1, 0)
    go(first1)

    band = 256

    def contrib(i, carry):
        rows = pl.ds(pl.multiple_of((i // 4) * band, band), band)
        cols = pl.ds(pl.multiple_of((i % 4) * tile, tile), tile)
        part[rows, cols] = lax.dot_general(
            dgu_ref[rows, :], w_ref[cols, :], (((1,), (1,)), ((), ())), preferred_element_type=f32
        ).astype(bf16)
        return carry

    lax.fori_loop(0, part.shape[0] // band * 4, contrib, 0)
    ring_step(0)
    weight_grads(xn, 0)
    keep0 = first(xn, 0, 1)
    go(keep0)
    weight_grads(yn, 1)
    keep1 = first(yn, 1, 1)
    go(keep1)
    ring_step(1)
    weight_grads(yn, 0)
    weight_grads(xn, 1)
    ring_step(2)
    for half, (block, copies) in enumerate(((yn, first0), (xn, first1))):
        copies[0].wait_recv()
        copies[1].wait_recv()
        g_gu[block, half] = (g_gu[block, half].astype(f32) + r1_gu[half, 0].astype(f32)).astype(bf16)
        g_d[block, half] = (g_d[block, half].astype(f32) + r1_d[half, 0].astype(f32)).astype(bf16)
        go(second(block, half))
    ring_step(3)
    weight_grads(me, 0)
    ring_step(4)
    weight_grads(me, 1)
    for s in range(5, n - 1):
        ring_step(s)
    for way in range(2):
        ring_copy(n - 2, way).wait_recv()
        rows = pl.ds(pl.multiple_of(q * tok + way * hrow, hrow), hrow)
        in_ref[pl.ds(way * hrow, hrow), :] = (
            part[rows].astype(f32) + landed[way, n - 2].astype(f32)).astype(bf16)
    for half, copies in enumerate((keep0, keep1)):
        copies[0].wait_recv()
        copies[1].wait_recv()
        last = second(yn if half == 0 else xn, half)
        last[0].wait_recv()
        out_gu[half] = (g_gu[me, half].astype(f32) + r1_gu[half, 1].astype(f32)
                        + r2_gu[half].astype(f32)).astype(bf16)
        last[1].wait_recv()
        out_d[half] = (g_d[me, half].astype(f32) + r1_d[half, 1].astype(f32)
                       + r2_d[half].astype(f32)).astype(bf16)
    for copy in sends:
        copy.wait_send()
    for s in range(n - 1):
        for way in range(2):
            ring_copy(s, way).wait_send()


def reduce_call(xt, dy, dgu, actt, w_gu, n, tok):
    bf16 = jnp.bfloat16
    width, total = xt.shape
    gu = dgu.shape[1]
    hid = actt.shape[0]
    rows, cols = width // 8, width // 4
    vmem = pl.BlockSpec(memory_space=pltpu.VMEM)
    return pl.pallas_call(
        functools.partial(reduce_kernel, n),
        out_shape=(
            jax.ShapeDtypeStruct((tok, width), bf16),
            jax.ShapeDtypeStruct((2, rows, gu), bf16),
            jax.ShapeDtypeStruct((2, hid // 2, cols), bf16),
        ),
        in_specs=[vmem] * 5,
        out_specs=(vmem,) * 3,
        scratch_shapes=[
            pltpu.VMEM((4, 2, rows, gu), bf16),
            pltpu.VMEM((4, 2, hid // 2, cols), bf16),
            pltpu.VMEM((2, 2, rows, gu), bf16),
            pltpu.VMEM((2, 2, hid // 2, cols), bf16),
            pltpu.VMEM((2, rows, gu), bf16),
            pltpu.VMEM((2, hid // 2, cols), bf16),
            pltpu.VMEM((total, width), bf16),
            pltpu.VMEM((2, n - 1, tok // 2, width), bf16),
            pltpu.SemaphoreType.DMA((2, 2, 2)),
            pltpu.SemaphoreType.DMA((2, 2, 2)),
            pltpu.SemaphoreType.DMA((2, 2)),
            pltpu.SemaphoreType.DMA((2, 2)),
            pltpu.SemaphoreType.DMA((2, n - 1)),
            pltpu.SemaphoreType.DMA((2, n - 1)),
        ],
        compiler_params=pltpu.CompilerParams(
            collective_id=0, has_side_effects=True, vmem_limit_bytes=60 * 1024 * 1024
        ),
    )(xt, dy, dgu, actt, w_gu)


def per_device(tokens, out_grad, expert_ids, route_probs, gate_weight, up_weight, down_weight):
    width = tokens.shape[1]
    exp_dev, _, hid = gate_weight.shape
    bf16 = jnp.bfloat16
    n_owner = lax.axis_size("expert")
    experts = exp_dev * n_owner
    columns = jnp.arange(experts, dtype=jnp.int32)
    hit = expert_ids[:, :, None] == columns[None, None, :]
    weight = jnp.sum(jnp.where(hit, route_probs[:, :, None], 0.0), axis=1)
    first = lax.axis_index("expert") * exp_dev
    all_weight = lax.all_gather(weight, "expert", axis=0, tiled=True)
    mine = lax.dynamic_slice_in_dim(all_weight, first, exp_dev, axis=1)
    x = lax.all_gather(tokens, "expert", axis=0, tiled=True)
    dy = lax.all_gather(out_grad, "expert", axis=0, tiled=True)
    w_gate = jnp.concatenate([gate_weight[e] for e in range(exp_dev)], axis=1)
    w_up = jnp.concatenate([up_weight[e] for e in range(exp_dev)], axis=1)
    w_down = down_weight.reshape(exp_dev * hid, width)
    prob = jnp.repeat(mine, hid, axis=1)
    gate = contract(x, w_gate, 1, 0)
    up = contract(x, w_up, 1, 0)
    sig = jax.nn.sigmoid(gate)
    silu = gate * sig
    slope = up * sig * (1.0 + gate * (1.0 - sig))
    dh = contract(dy, w_down, 1, 1) * prob
    act = (silu * up * prob).astype(bf16)
    dgate = (dh * slope).astype(bf16)
    dup = (dh * silu).astype(bf16)
    if exp_dev == 2 and lax.axis_size("dp") == 4 and n_owner == 8:
        in_grad, gu, down = reduce_call(
            x.T, dy, jnp.concatenate([dgate, dup], axis=1), act.T,
            jnp.concatenate([w_gate, w_up], axis=1), n_owner, tokens.shape[0],
        )
        gu = gu.reshape(width // 4, 2, exp_dev, hid)
        grad_g, grad_u = (gu[:, k].transpose(1, 0, 2) for k in range(2))
        return (in_grad, grad_g, grad_u, down)
    grad_d = contract(act, dy, 0, 0).astype(bf16).reshape(exp_dev, hid, width)
    grad_g = contract(x, dgate, 0, 0).astype(bf16)
    grad_u = contract(x, dup, 0, 0).astype(bf16)
    grad_g = jnp.stack([grad_g[:, e * hid:(e + 1) * hid] for e in range(exp_dev)], axis=0)
    grad_u = jnp.stack([grad_u[:, e * hid:(e + 1) * hid] for e in range(exp_dev)], axis=0)
    part = (contract(dgate, w_gate, 1, 1) + contract(dup, w_up, 1, 1)).astype(bf16)
    in_grad = lax.psum_scatter(part, "expert", scatter_dimension=0, tiled=True)
    grad_d = lax.psum_scatter(grad_d, "dp", scatter_dimension=2, tiled=True)
    grad_g = lax.psum_scatter(grad_g, "dp", scatter_dimension=1, tiled=True)
    grad_u = lax.psum_scatter(grad_u, "dp", scatter_dimension=1, tiled=True)
    return (in_grad, grad_g, grad_u, grad_d)


def solution(mesh):
    in_specs = (
        P(("dp", "expert"), None),
        P(("dp", "expert"), None),
        P(("dp", "expert"), None),
        P(("dp", "expert"), None),
        P("expert", None, None),
        P("expert", None, None),
        P("expert", None, None),
    )
    out_specs = (
        P(("dp", "expert"), None),
        P("expert", "dp", None),
        P("expert", "dp", None),
        P("expert", None, "dp"),
    )
    return jax.shard_map(
        per_device, mesh=mesh, in_specs=in_specs, out_specs=out_specs, check_vma=False
    )
```

```python
import functools

import jax
import jax.numpy as jnp
from jax import lax
from jax.experimental import pallas as pl
from jax.experimental.pallas import tpu as pltpu
from jax.sharding import PartitionSpec as P


def contract(left, right, left_dim, right_dim):
    return lax.dot_general(
        left, right, (((left_dim,), (right_dim,)), ((), ())), preferred_element_type=jnp.float32
    )


MESH = pl.DeviceIdType.MESH


def ring_owner(place, n):
    return jnp.where(place < n // 2, 2 * place, 2 * (n - 1 - place) + 1)


def reduce_kernel(
    n, xt_ref, dy_ref, dgu_ref, actt_ref, w_ref,
    in_ref, out_g, out_u, out_d,
    g_gu, g_d, r1_gu, r1_d, r2_gu, r2_d, part, landed,
    s1_send, s1_recv, s2_send, s2_recv, ring_send, ring_recv,
):
    f32, bf16 = jnp.float32, jnp.bfloat16
    me = lax.axis_index("dp")
    q = lax.axis_index("expert")
    xx, yy = me % 2, me // 2
    xn = yy * 2 + (1 - xx)
    yn = (1 - yy) * 2 + xx
    diag = 3 - me
    place = jnp.where(q % 2 == 0, q // 2, n - 1 - q // 2)
    right = ring_owner((place + 1) % n, n)
    left = ring_owner((place + n - 1) % n, n)

    barrier = pltpu.get_barrier_semaphore()
    for target in ((xn, q), (yn, q), (me, right), (me, left)):
        pl.semaphore_signal(barrier, inc=1, device_id=target, device_id_type=MESH)
    pl.semaphore_wait(barrier, 4)

    gu_rows, gu_cols = g_gu.shape[2:]
    d_rows, d_cols = g_d.shape[2:]
    tile = 512

    def weight_grads(block, half):
        rows = pl.multiple_of((block * 2 + half) * gu_rows, gu_rows)

        def step(i, carry):
            cols = pl.ds(pl.multiple_of(i * tile, tile), tile)
            g_gu[block, half, :, cols] = jnp.dot(
                xt_ref[pl.ds(rows, gu_rows), :], dgu_ref[:, cols], preferred_element_type=f32
            ).astype(bf16)
            return carry

        lax.fori_loop(0, gu_cols // tile, step, 0)
        g_d[block, half] = jnp.dot(
            actt_ref[pl.ds(half * d_rows, d_rows), :],
            dy_ref[:, pl.ds(pl.multiple_of(block * d_cols, d_cols), d_cols)],
            preferred_element_type=f32,
        ).astype(bf16)

    def first(block, half, slot):
        target = (xn, q) if half == 0 else (yn, q)
        copies = []
        for kind, (src, dst) in enumerate(((g_gu, r1_gu), (g_d, r1_d))):
            copies.append(pltpu.make_async_remote_copy(
                src_ref=src.at[block, half], dst_ref=dst.at[half, slot],
                send_sem=s1_send.at[half, slot, kind], recv_sem=s1_recv.at[half, slot, kind],
                device_id=target, device_id_type=MESH))
        return copies

    def second(block, half):
        target = (yn, q) if half == 0 else (xn, q)
        copies = []
        for kind, (src, dst) in enumerate(((g_gu, r2_gu), (g_d, r2_d))):
            copies.append(pltpu.make_async_remote_copy(
                src_ref=src.at[block, half], dst_ref=dst.at[half],
                send_sem=s2_send.at[half, kind], recv_sem=s2_recv.at[half, kind],
                device_id=target, device_id_type=MESH))
        return copies

    tok = in_ref.shape[0]
    hrow = tok // 2

    def ring_rows(s, way):
        if way == 0:
            owner = ring_owner((place + 2 * n - 1 - s) % n, n)
        else:
            owner = ring_owner((place + 1 + s) % n, n)
        return pl.ds(pl.multiple_of(owner * tok + way * hrow, hrow), hrow)

    def ring_copy(s, way):
        return pltpu.make_async_remote_copy(
            src_ref=part.at[ring_rows(s, way)], dst_ref=landed.at[way, s],
            send_sem=ring_send.at[way, s], recv_sem=ring_recv.at[way, s],
            device_id=(me, right if way == 0 else left), device_id_type=MESH)

    def ring_step(s):
        for way in range(2):
            if s > 0:
                ring_copy(s - 1, way).wait_recv()
                rows = ring_rows(s, way)
                part[rows] = (part[rows].astype(f32) + landed[way, s - 1].astype(f32)).astype(bf16)
            ring_copy(s, way).start()

    sends = []

    def go(copies):
        for copy in copies:
            copy.start()
        sends.extend(copies)

    weight_grads(diag, 0)
    first0 = first(diag, 0, 0)
    go(first0)
    weight_grads(diag, 1)
    first1 = first(diag, 1, 0)
    go(first1)

    band = 256

    def contrib(i, carry):
        rows = pl.ds(pl.multiple_of((i // 4) * band, band), band)
        cols = pl.ds(pl.multiple_of((i % 4) * tile, tile), tile)
        part[rows, cols] = lax.dot_general(
            dgu_ref[rows, :], w_ref[cols, :], (((1,), (1,)), ((), ())), preferred_element_type=f32
        ).astype(bf16)
        return carry

    lax.fori_loop(0, part.shape[0] // band * 4, contrib, 0)
    ring_step(0)
    weight_grads(xn, 0)
    keep0 = first(xn, 0, 1)
    go(keep0)
    weight_grads(yn, 1)
    keep1 = first(yn, 1, 1)
    go(keep1)
    ring_step(1)
    weight_grads(yn, 0)
    weight_grads(xn, 1)
    ring_step(2)
    for half, (block, copies) in enumerate(((yn, first0), (xn, first1))):
        copies[0].wait_recv()
        copies[1].wait_recv()
        g_gu[block, half] = (g_gu[block, half].astype(f32) + r1_gu[half, 0].astype(f32)).astype(bf16)
        g_d[block, half] = (g_d[block, half].astype(f32) + r1_d[half, 0].astype(f32)).astype(bf16)
        go(second(block, half))
    ring_step(3)
    weight_grads(me, 0)
    ring_step(4)
    weight_grads(me, 1)
    for s in range(5, n - 1):
        ring_step(s)
    for way in range(2):
        ring_copy(n - 2, way).wait_recv()
        rows = pl.ds(pl.multiple_of(q * tok + way * hrow, hrow), hrow)
        in_ref[pl.ds(way * hrow, hrow), :] = (
            part[rows].astype(f32) + landed[way, n - 2].astype(f32)).astype(bf16)
    for half, copies in enumerate((keep0, keep1)):
        copies[0].wait_recv()
        copies[1].wait_recv()
        last = second(yn if half == 0 else xn, half)
        last[0].wait_recv()
        whole = (g_gu[me, half].astype(f32) + r1_gu[half, 1].astype(f32)
                 + r2_gu[half].astype(f32)).astype(bf16)
        hid = out_g.shape[2]
        for e in range(2):
            rows = slice(half * gu_rows, (half + 1) * gu_rows)
            out_g[e, rows, :] = whole[:, e * hid:(e + 1) * hid]
            out_u[e, rows, :] = whole[:, (2 + e) * hid:(3 + e) * hid]
        last[1].wait_recv()
        out_d[half] = (g_d[me, half].astype(f32) + r1_d[half, 1].astype(f32)
                       + r2_d[half].astype(f32)).astype(bf16)
    for copy in sends:
        copy.wait_send()
    for s in range(n - 1):
        for way in range(2):
            ring_copy(s, way).wait_send()


def reduce_call(xt, dy, dgu, actt, w_gu, n, tok):
    bf16 = jnp.bfloat16
    width, total = xt.shape
    gu = dgu.shape[1]
    hid = actt.shape[0]
    rows, cols = width // 8, width // 4
    vmem = pl.BlockSpec(memory_space=pltpu.VMEM)
    return pl.pallas_call(
        functools.partial(reduce_kernel, n),
        out_shape=(
            jax.ShapeDtypeStruct((tok, width), bf16),
            jax.ShapeDtypeStruct((2, 2 * rows, gu // 4), bf16),
            jax.ShapeDtypeStruct((2, 2 * rows, gu // 4), bf16),
            jax.ShapeDtypeStruct((2, hid // 2, cols), bf16),
        ),
        in_specs=[vmem] * 5,
        out_specs=(vmem,) * 4,
        scratch_shapes=[
            pltpu.VMEM((4, 2, rows, gu), bf16),
            pltpu.VMEM((4, 2, hid // 2, cols), bf16),
            pltpu.VMEM((2, 2, rows, gu), bf16),
            pltpu.VMEM((2, 2, hid // 2, cols), bf16),
            pltpu.VMEM((2, rows, gu), bf16),
            pltpu.VMEM((2, hid // 2, cols), bf16),
            pltpu.VMEM((total, width), bf16),
            pltpu.VMEM((2, n - 1, tok // 2, width), bf16),
            pltpu.SemaphoreType.DMA((2, 2, 2)),
            pltpu.SemaphoreType.DMA((2, 2, 2)),
            pltpu.SemaphoreType.DMA((2, 2)),
            pltpu.SemaphoreType.DMA((2, 2)),
            pltpu.SemaphoreType.DMA((2, n - 1)),
            pltpu.SemaphoreType.DMA((2, n - 1)),
        ],
        compiler_params=pltpu.CompilerParams(
            collective_id=0, has_side_effects=True, vmem_limit_bytes=60 * 1024 * 1024
        ),
    )(xt, dy, dgu, actt, w_gu)


def gather_kernel(
    n, tok_ref, own_dy_ref, own_wt_ref, w_ref, wd_ref,
    x_ref, dy_ref, dgu_ref, act_ref, wt_ref, send, recv,
):
    f32, bf16 = jnp.float32, jnp.bfloat16
    me = lax.axis_index("dp")
    q = lax.axis_index("expert")
    place = jnp.where(q % 2 == 0, q // 2, n - 1 - q // 2)
    right = ring_owner((place + 1) % n, n)
    left = ring_owner((place + n - 1) % n, n)
    tok = tok_ref.shape[0]
    hrow = tok // 2
    hid = wd_ref.shape[0] // 2
    arrays = (x_ref, dy_ref, wt_ref)

    own = pl.ds(pl.multiple_of(q * tok, tok), tok)
    x_ref[own, :] = tok_ref[...]
    dy_ref[own, :] = own_dy_ref[...]
    wt_ref[own, :] = own_wt_ref[...]

    barrier = pltpu.get_barrier_semaphore()
    for target in ((me, right), (me, left)):
        pl.semaphore_signal(barrier, inc=1, device_id=target, device_id_type=MESH)
    pl.semaphore_wait(barrier, 2)

    def rows_of(s, way):
        owner = ring_owner((place + n - s) % n if way == 0 else (place + s) % n, n)
        return pl.ds(pl.multiple_of(owner * tok + way * hrow, hrow), hrow)

    def copy(kind, s, way, slot):
        rows = rows_of(s, way)
        return pltpu.make_async_remote_copy(
            src_ref=arrays[kind].at[rows], dst_ref=arrays[kind].at[rows],
            send_sem=send.at[way, slot, kind], recv_sem=recv.at[way, slot, kind],
            device_id=(me, right if way == 0 else left), device_id_type=MESH)

    def step(s, carry):
        @pl.when(s > 0)
        def _():
            for kind in range(3):
                for way in range(2):
                    copy(kind, s, way, s - 1).wait_recv()

        @pl.when(s < n - 1)
        def _():
            for kind in range(3):
                for way in range(2):
                    copy(kind, s, way, s).start()

        first, second = rows_of(s, 0), rows_of(s, 1)
        xb = jnp.concatenate([x_ref[first, :], x_ref[second, :]], axis=0)
        dyb = jnp.concatenate([dy_ref[first, :], dy_ref[second, :]], axis=0)
        wt = jnp.concatenate([wt_ref[first, :], wt_ref[second, :]], axis=0)
        lane = lax.broadcasted_iota(jnp.int32, wt.shape, 1)
        for e in range(2):
            prob = jnp.sum(jnp.where(lane == 2 * q + e, wt, 0.0), axis=1, keepdims=True)
            lo, hi = e * hid, (e + 1) * hid
            gate = jnp.dot(xb, w_ref[:, lo:hi], preferred_element_type=f32)
            up = jnp.dot(xb, w_ref[:, 2 * hid + lo:2 * hid + hi], preferred_element_type=f32)
            dh = prob * lax.dot_general(
                dyb, wd_ref[lo:hi, :], (((1,), (1,)), ((), ())), preferred_element_type=f32)
            sig = jax.nn.sigmoid(gate)
            silu = gate * sig
            act = (silu * up * prob).astype(bf16)
            dgate = (dh * up * sig * (1.0 + gate * (1.0 - sig))).astype(bf16)
            dup = (dh * silu).astype(bf16)
            for rows, a in ((first, 0), (second, hrow)):
                act_ref[rows, lo:hi] = act[a:a + hrow]
                dgu_ref[rows, lo:hi] = dgate[a:a + hrow]
                dgu_ref[rows, 2 * hid + lo:2 * hid + hi] = dup[a:a + hrow]
        return carry

    lax.fori_loop(0, n, step, 0)

    def drain(s, carry):
        for kind in range(3):
            for way in range(2):
                copy(kind, s, way, s).wait_send()
        return carry

    lax.fori_loop(0, n - 1, drain, 0)


def gather_call(tokens, out_grad, weight, w_gu, w_down, n):
    bf16 = jnp.bfloat16
    tok, width = tokens.shape
    total = n * tok
    weight = jnp.pad(weight, ((0, 0), (0, 128 - weight.shape[1])))
    vmem = pl.BlockSpec(memory_space=pltpu.VMEM)
    return pl.pallas_call(
        functools.partial(gather_kernel, n),
        out_shape=(
            jax.ShapeDtypeStruct((total, width), bf16),
            jax.ShapeDtypeStruct((total, width), bf16),
            jax.ShapeDtypeStruct((total, w_gu.shape[1]), bf16),
            jax.ShapeDtypeStruct((total, w_down.shape[0]), bf16),
        ),
        in_specs=[vmem] * 5,
        out_specs=(vmem,) * 4,
        scratch_shapes=[
            pltpu.VMEM((total, 128), jnp.float32),
            pltpu.SemaphoreType.DMA((2, n - 1, 3)),
            pltpu.SemaphoreType.DMA((2, n - 1, 3)),
        ],
        compiler_params=pltpu.CompilerParams(
            collective_id=1, has_side_effects=True, vmem_limit_bytes=48 * 1024 * 1024
        ),
    )(tokens, out_grad, weight, w_gu, w_down)


def per_device(tokens, out_grad, expert_ids, route_probs, gate_weight, up_weight, down_weight):
    width = tokens.shape[1]
    exp_dev, _, hid = gate_weight.shape
    bf16 = jnp.bfloat16
    n_owner = lax.axis_size("expert")
    experts = exp_dev * n_owner
    columns = jnp.arange(experts, dtype=jnp.int32)
    hit = expert_ids[:, :, None] == columns[None, None, :]
    weight = jnp.sum(jnp.where(hit, route_probs[:, :, None], 0.0), axis=1)
    w_gate = jnp.concatenate([gate_weight[e] for e in range(exp_dev)], axis=1)
    w_up = jnp.concatenate([up_weight[e] for e in range(exp_dev)], axis=1)
    w_down = down_weight.reshape(exp_dev * hid, width)
    if exp_dev == 2 and lax.axis_size("dp") == 4 and n_owner == 8:
        w_gu = jnp.concatenate([w_gate, w_up], axis=1)
        x, dy, dgu, act = gather_call(tokens, out_grad, weight, w_gu, w_down, n_owner)
        return reduce_call(x.T, dy, dgu, act.T, w_gu, n_owner, tokens.shape[0])
    first = lax.axis_index("expert") * exp_dev
    all_weight = lax.all_gather(weight, "expert", axis=0, tiled=True)
    mine = lax.dynamic_slice_in_dim(all_weight, first, exp_dev, axis=1)
    x = lax.all_gather(tokens, "expert", axis=0, tiled=True)
    dy = lax.all_gather(out_grad, "expert", axis=0, tiled=True)
    prob = jnp.repeat(mine, hid, axis=1)
    gate = contract(x, w_gate, 1, 0)
    up = contract(x, w_up, 1, 0)
    sig = jax.nn.sigmoid(gate)
    silu = gate * sig
    slope = up * sig * (1.0 + gate * (1.0 - sig))
    dh = contract(dy, w_down, 1, 1) * prob
    act = (silu * up * prob).astype(bf16)
    dgate = (dh * slope).astype(bf16)
    dup = (dh * silu).astype(bf16)
    grad_d = contract(act, dy, 0, 0).astype(bf16).reshape(exp_dev, hid, width)
    grad_g = contract(x, dgate, 0, 0).astype(bf16)
    grad_u = contract(x, dup, 0, 0).astype(bf16)
    grad_g = jnp.stack([grad_g[:, e * hid:(e + 1) * hid] for e in range(exp_dev)], axis=0)
    grad_u = jnp.stack([grad_u[:, e * hid:(e + 1) * hid] for e in range(exp_dev)], axis=0)
    part = (contract(dgate, w_gate, 1, 1) + contract(dup, w_up, 1, 1)).astype(bf16)
    in_grad = lax.psum_scatter(part, "expert", scatter_dimension=0, tiled=True)
    grad_d = lax.psum_scatter(grad_d, "dp", scatter_dimension=2, tiled=True)
    grad_g = lax.psum_scatter(grad_g, "dp", scatter_dimension=1, tiled=True)
    grad_u = lax.psum_scatter(grad_u, "dp", scatter_dimension=1, tiled=True)
    return (in_grad, grad_g, grad_u, grad_d)


def solution(mesh):
    in_specs = (
        P(("dp", "expert"), None),
        P(("dp", "expert"), None),
        P(("dp", "expert"), None),
        P(("dp", "expert"), None),
        P("expert", None, None),
        P("expert", None, None),
        P("expert", None, None),
    )
    out_specs = (
        P(("dp", "expert"), None),
        P("expert", "dp", None),
        P("expert", "dp", None),
        P("expert", None, "dp"),
    )
    return jax.shard_map(
        per_device, mesh=mesh, in_specs=in_specs, out_specs=out_specs, check_vma=False
    )
```
